1024 devices in a mesh: gx: 8 (over z_lo), gy: 16 (over y, z_hi), gz: 8 (over x, core).
Axes of the slice: x: 4, y: 4, z: 32 (z_hi: 4, z_lo: 8; z = z_hi * 8 + z_lo), core: 2. Of those that a mesh axis runs over, the one named last changes fastest.
Arguments:
- fine_residual: bfloat16 [8, 16, 8, 2, 2, 12, 32, 256], P('gx', 'gy', 'gz'), may hold values from -6 to 6
- candidates: bfloat16 [8, 16, 8, 2, 48, 2, 12, 256], P('gx', 'gy', 'gz'), may hold values from -0.29882812 to 0.29882812
- vector_pick: int32 [32], replicated, may hold values from 0 to 47, as said below
- coarse_links: float32 [8, 16, 8, 2, 9, 64, 128], P(None, 'gy', 'gz'), may hold values from -0.1875 to 0.1875
Outputs:
- correction: bfloat16 [8, 16, 8, 2, 2, 12, 32, 256], P('gx', 'gy', 'gz')
- coarse_error: float32 [8, 16, 8, 2, 2, 64, 32], P('gx', 'gy', 'gz')
The draws below stay inside these ranges and needn't reach their ends.
Inputs may be any that keep to these rules, and one draw needn't show every extreme that they name: `vector_pick`: 32 distinct indices of candidate vectors.
All inputs are finite; a program needn't handle non-finite values.
Results may differ from the reference program's by a relative error of at most 0.0049.
Values sent between devices are 32-bit elements; how exact they have to be, the bound alone decides.
A program may use at most 32 MiB of HBM per device.

```python
import jax
import jax.numpy as jnp
from jax import lax

DOF = 12
NV = 32
POOL = 48
BSITES = 256
TB = 2
RHS = 32
APPLIES = 2
NC = 64
CX = 8
CY = 16
CZ = 8


def draw_vector_pick(key, part):
    key = jax.random.fold_in(key, 7)
    inner_key, order_key = jax.random.split(key)
    middle = jax.random.permutation(inner_key, POOL - 2)[:NV - 2] + 1
    picked = jnp.concatenate([jnp.array([0, POOL - 1], dtype=jnp.int32), middle.astype(jnp.int32)])
    return jax.random.permutation(order_key, picked).astype(jnp.int32)


def level_of(rng, extent, shards, low, high):
    def one(dim, shards_of):
        steps = jax.random.uniform(jax.random.fold_in(jax.random.fold_in(rng, 6), dim), (shards_of,), jnp.float32, low / len(shards), high / len(shards))
        return jnp.repeat(jnp.exp(steps), extent[dim] // shards_of).reshape((-1,) + (1,) * (len(extent) - dim - 1))

    factor_of = one(*shards[0])
    for cut in shards[1:]:
        factor_of = factor_of * one(*cut)
    return factor_of


def noise(own_key, dims, spread, limit, cuts=(), kind=jnp.bfloat16):
    values = jax.random.normal(own_key, dims, jnp.float32) * spread
    if len(cuts) > 0:
        values = level_of(own_key, dims, cuts, -0.22, 0.18) * values
    return jnp.clip(values, min=-limit, max=limit).astype(kind)


def setup_inputs(seed: int = 0) -> dict:
    seeds = jax.random.split(jax.random.key(seed), 5)
    return {
        "fine_residual": noise(seeds[0], (CX, CY, CZ, TB, 2, DOF, RHS, BSITES), 1.0, 6.0, ((0, 8), (1, 16), (2, 8))),
        "candidates": noise(seeds[1], (CX, CY, CZ, TB, POOL, 2, DOF, BSITES), 0.05, 0.29882812, ((0, 8), (1, 16), (2, 8))),
        "vector_pick": draw_vector_pick(jax.random.fold_in(seeds[4], 71), 0),
        "coarse_links": noise(seeds[3], (CX, CY, CZ, TB, 9, NC, 2 * NC), (18 * NC) ** -0.5, 0.1875, ((1, 16), (2, 8)), jnp.float32),
    }


def complex_apply(matrix, vector):
    real_part = vector[..., 0, :, :]
    imag_part = vector[..., 1, :, :]
    columns = jnp.concatenate([jnp.concatenate([real_part, -imag_part], axis=-2), jnp.concatenate([imag_part, real_part], axis=-2)], axis=-1)
    product = jnp.einsum('...ij,...jr->...ir', matrix, columns, precision=lax.Precision.HIGHEST)
    split_at = real_part.shape[-1]
    return jnp.stack([product[..., :split_at], product[..., split_at:]], axis=-3)


def coarse_operator(coarse_links, vector):
    summed = vector + complex_apply(coarse_links[:, :, :, :, 0], vector)
    direction = 1
    for dimension in range(4):
        for step_sign in (-1, 1):
            summed = summed - complex_apply(coarse_links[:, :, :, :, direction], jnp.roll(vector, step_sign, dimension))
            direction = direction + 1
    return summed


def reference(fine_residual, candidates, vector_pick, coarse_links):
    groups = CX * CY
    fine_groups = fine_residual.reshape((groups, CZ, TB, 2, DOF, RHS, BSITES))
    pool_groups = candidates.reshape((groups, CZ, TB, POOL, 2, DOF, BSITES))

    def restrict_group(operands):
        fine_part, pool_part = operands
        chosen = jnp.take(pool_part, vector_pick, axis=2)
        shaped = chosen.reshape((CZ, TB, NV, 2, 2, DOF // 2, BSITES)).astype(jnp.float32)
        source = fine_part.reshape((CZ, TB, 2, 2, DOF // 2, RHS, BSITES)).astype(jnp.float32)
        partial_terms = jnp.einsum('...kqhcs,...phcrs->...hkqpr', shaped, source, precision=lax.Precision.HIGHEST)
        real_part = partial_terms[..., 0, 0, :] + partial_terms[..., 1, 1, :]
        imag_part = partial_terms[..., 0, 1, :] - partial_terms[..., 1, 0, :]
        return jnp.stack([real_part.reshape((CZ, TB, NC, RHS)), imag_part.reshape((CZ, TB, NC, RHS))], axis=2)

    restricted = lax.map(restrict_group, (fine_groups, pool_groups)).reshape((CX, CY, CZ, TB, 2, NC, RHS))
    coarse_error = 0.5 * restricted
    for repeat in range(APPLIES):
        coarse_error = coarse_error + 0.5 * (restricted - coarse_operator(coarse_links, coarse_error))
    error_half = coarse_error.astype(jnp.bfloat16)
    error_groups = error_half.reshape((groups, CZ, TB, 2, NC, RHS))

    def prolong_group(operands):
        error_part, pool_part = operands
        chosen = jnp.take(pool_part, vector_pick, axis=2)
        shaped = chosen.reshape((CZ, TB, NV, 2, 2, DOF // 2, BSITES)).astype(jnp.float32)
        coarse = error_part.reshape((CZ, TB, 2, 2, NV, RHS)).astype(jnp.float32)
        grid = jnp.einsum('...kqhcs,...phkr->...qphcrs', shaped, coarse, precision=lax.Precision.HIGHEST)
        real_part = grid[:, :, 0, 0] - grid[:, :, 1, 1]
        imag_part = grid[:, :, 0, 1] + grid[:, :, 1, 0]
        stacked = jnp.stack([real_part.reshape((CZ, TB, DOF, RHS, BSITES)), imag_part.reshape((CZ, TB, DOF, RHS, BSITES))], axis=2)
        return stacked.astype(jnp.bfloat16)

    correction = lax.map(prolong_group, (error_groups, pool_groups)).reshape((CX, CY, CZ, TB, 2, DOF, RHS, BSITES))
    return correction, coarse_error
```

```python
import functools

import jax
import jax.numpy as jnp
from jax import lax
from jax.experimental import pallas as pl
from jax.experimental.pallas import tpu as pltpu
from jax.sharding import PartitionSpec as P

NV = 32
POOL = 48
TB = 2
DOF = 12
HALF = DOF // 2
SITES = 256
RHS = 32
NC = 64
LANES = 2 * NC
CHUNKS = 4
ROWS = RHS // CHUNKS
SIDES = (
    ("gx", 1, 1),
    ("gx", -1, 2),
    ("gz", 1, 5),
    ("gz", -1, 6),
    ("gy", 1, 3),
    ("gy", -1, 4),
)
SEND_ORDER = (4, 5, 0, 1, 2, 3)
NEAR = 6
NT = (((1,), (1,)), ((), ()))
NN = (((1,), (0,)), ((), ()))


def dot(a, b, dims):
    return lax.dot_general(a, b, dims, preferred_element_type=jnp.float32)


def step_on(axis, step, size):
    return lax.rem(lax.axis_index(axis) + (step + size), size)


def picked(pick_ref, p, h):
    lane = lax.broadcasted_iota(jnp.int32, (2 * POOL, LANES), 1)
    row = lax.broadcasted_iota(jnp.int32, (2 * POOL, LANES), 0)
    wanted = jnp.zeros((2 * POOL, LANES), jnp.int32)
    for k in range(NV):
        wanted = jnp.where((lane & (NV - 1)) == k, pick_ref[k], wanted)
    part = row & 1
    hit = (row >> 1 == wanted) & (((lane >> 5) & 1) == h) & ((part ^ p) == lane >> 6)
    sign = jnp.where((part == 1) & (p == 0), -1.0, 1.0)
    return jnp.where(hit, sign, 0.0).astype(jnp.bfloat16)


def kernel(
    sizes,
    pick_ref,
    fine_ref,
    cand_ref,
    links_ref,
    corr_ref,
    err_ref,
    fine_v,
    cand_v,
    chosen_v,
    links_v,
    oper_v,
    rhs_v,
    mid_v,
    got_v,
    error_v,
    corr_v,
    in_sem,
    out_sem,
    send_sem,
    recv_sem,
):
    loads = []
    for t in range(TB):
        loads.append(pltpu.make_async_copy(cand_ref.at[t], cand_v.at[t], in_sem.at[2 * t]))
        loads.append(pltpu.make_async_copy(fine_ref.at[t], fine_v.at[t], in_sem.at[2 * t + 1]))
    loads.append(pltpu.make_async_copy(links_ref.at[lax.axis_index("gx")], links_v, in_sem.at[4]))
    for load in loads:
        load.start()

    barrier = pltpu.get_barrier_semaphore()
    for axis, step, _ in SIDES:
        pl.semaphore_signal(
            barrier,
            inc=1,
            device_id={axis: step_on(axis, step, sizes[axis])},
            device_id_type=pl.DeviceIdType.MESH,
        )

    def transfer(turn, chunk, side):
        axis, step, _ = SIDES[side]
        return pltpu.make_async_remote_copy(
            src_ref=(rhs_v, mid_v)[turn].at[chunk],
            dst_ref=got_v.at[turn, side, chunk],
            send_sem=send_sem.at[turn, chunk, side],
            recv_sem=recv_sem.at[turn, chunk, side],
            device_id={axis: step_on(axis, -step, sizes[axis])},
            device_id_type=pl.DeviceIdType.MESH,
        )

    select = [[picked(pick_ref, p, h) for h in range(2)] for p in range(2)]

    for t in range(TB):
        loads[2 * t].wait()
        loads[2 * t + 1].wait()
        total = jnp.zeros((RHS, LANES), jnp.float32)
        for h in range(2):
            some = range(h * HALF, (h + 1) * HALF)
            for a in some:
                chosen_v[t, a] = cand_v[t, :, a].reshape(2 * POOL, SITES)
            vectors = jnp.concatenate([chosen_v[t, a] for a in some], axis=1)
            field = jnp.concatenate([fine_v[t, :, a].reshape(2 * RHS, SITES) for a in some], axis=1)
            terms = dot(field, vectors, NT)
            high = terms.astype(jnp.bfloat16)
            rest = terms - high.astype(jnp.float32)
            low = rest.astype(jnp.bfloat16)
            lowest = (rest - low.astype(jnp.float32)).astype(jnp.bfloat16)
            for p in range(2):
                here = slice(p * RHS, (p + 1) * RHS)
                for piece in (high, low, lowest):
                    total = total + dot(piece[here], select[p][h], NN)
        for c in range(CHUNKS):
            rhs_v[c, t] = total[c * ROWS : (c + 1) * ROWS]

    pl.semaphore_wait(barrier, len(SIDES))
    for c in range(CHUNKS):
        for side in SEND_ORDER:
            transfer(0, c, side).start()

    loads[4].wait()
    lane = lax.broadcasted_iota(jnp.int32, (NC, LANES), 1)
    for t in range(TB):
        blocks = [links_v[t, 0], -(links_v[t, 7] + links_v[t, 8])]
        blocks = blocks + [-links_v[t, link] for _, _, link in SIDES]
        for i, block in enumerate(blocks):
            columns = slice(i * LANES, (i + 1) * LANES)
            oper_v[t, :NC, columns] = jnp.where(lane < NC, block, -block).astype(jnp.bfloat16)
            oper_v[t, NC:, columns] = pltpu.roll(block, NC, 1).astype(jnp.bfloat16)

    def image(turn, c):
        vector = (rhs_v, mid_v)[turn]
        own = [vector[c, t].astype(jnp.bfloat16) for t in range(TB)]
        parts = []
        for side in range(len(SIDES)):
            transfer(turn, c, side).wait_recv()
        for t in range(TB):
            row = [own[t], own[1 - t]]
            row = row + [got_v[turn, side, c, t].astype(jnp.bfloat16) for side in range(len(SIDES))]
            parts.append(dot(jnp.concatenate(row, axis=1), oper_v[t], NT))
        return parts

    for c in range(CHUNKS):
        found = image(0, c)
        for t in range(TB):
            mid_v[c, t] = 0.75 * rhs_v[c, t] - 0.25 * found[t]
        for side in SEND_ORDER:
            transfer(1, c, side).start()

    for c in range(CHUNKS):
        found = image(1, c)
        rows = slice(c * ROWS, (c + 1) * ROWS)
        for t in range(TB):
            error = 0.5 * (mid_v[c, t] + rhs_v[c, t] - found[t])
            error_v[t, rows] = error
            err_ref[t, 0, rows] = error[:, :NC]
            err_ref[t, 1, rows] = error[:, NC:]

    stores = []
    for t in range(TB):
        error_half = error_v[t].astype(jnp.bfloat16)
        for h in range(2):
            factor = jnp.concatenate([dot(error_half, select[q][h], NT) for q in range(2)], axis=0)
            factor = factor.astype(jnp.bfloat16)
            for a in range(h * HALF, (h + 1) * HALF):
                out = dot(factor, chosen_v[t, a], NN).astype(jnp.bfloat16)
                corr_v[t, 0, a] = out[:RHS]
                corr_v[t, 1, a] = out[RHS:]
        store = pltpu.make_async_copy(corr_v.at[t], corr_ref.at[t], out_sem.at[t])
        store.start()
        stores.append(store)

    for turn in range(2):
        for c in range(CHUNKS):
            for side in range(len(SIDES)):
                transfer(turn, c, side).wait_send()
    for store in stores:
        store.wait()


def on_device(sizes, fine_residual, candidates, vector_pick, coarse_links):
    fine = fine_residual[0, 0, 0]
    pool = jnp.swapaxes(candidates[0, 0, 0], 2, 3)
    links = coarse_links[:, 0, 0]
    hbm = pl.BlockSpec(memory_space=pltpu.HBM)
    sides = len(SIDES)
    correction, error = pl.pallas_call(
        functools.partial(kernel, sizes),
        out_shape=(
            jax.ShapeDtypeStruct((TB, 2, DOF, RHS, SITES), jnp.bfloat16),
            jax.ShapeDtypeStruct((TB, 2, RHS, NC), jnp.float32),
        ),
        in_specs=[pl.BlockSpec(memory_space=pltpu.SMEM), hbm, hbm, hbm],
        out_specs=(hbm, pl.BlockSpec(memory_space=pltpu.VMEM)),
        scratch_shapes=[
            pltpu.VMEM((TB, 2, DOF, RHS, SITES), jnp.bfloat16),
            pltpu.VMEM((TB, POOL, DOF, 2, SITES), jnp.bfloat16),
            pltpu.VMEM((TB, DOF, 2 * POOL, SITES), jnp.bfloat16),
            pltpu.VMEM((TB, 9, NC, LANES), jnp.float32),
            pltpu.VMEM((TB, LANES, 8 * LANES), jnp.bfloat16),
            pltpu.VMEM((CHUNKS, TB, ROWS, LANES), jnp.float32),
            pltpu.VMEM((CHUNKS, TB, ROWS, LANES), jnp.float32),
            pltpu.VMEM((2, sides, CHUNKS, TB, ROWS, LANES), jnp.float32),
            pltpu.VMEM((TB, RHS, LANES), jnp.float32),
            pltpu.VMEM((TB, 2, DOF, RHS, SITES), jnp.bfloat16),
            pltpu.SemaphoreType.DMA((5,)),
            pltpu.SemaphoreType.DMA((TB,)),
            pltpu.SemaphoreType.DMA((2, CHUNKS, sides)),
            pltpu.SemaphoreType.DMA((2, CHUNKS, sides)),
        ],
        compiler_params=pltpu.CompilerParams(
            collective_id=0, has_side_effects=True, vmem_limit_bytes=48 << 20
        ),
        name="coarse_correction",
    )(vector_pick, fine, pool, links)
    return (correction[None, None, None], jnp.swapaxes(error, 2, 3)[None, None, None])


def solution(mesh):
    placed = (
        P("gx", "gy", "gz", None, None, None, None, None),
        P("gx", "gy", "gz", None, None, None, None, None),
        P(),
        P(None, "gy", "gz", None, None, None, None),
    )
    return jax.shard_map(
        functools.partial(on_device, dict(mesh.shape)),
        mesh=mesh,
        in_specs=placed,
        out_specs=(
            P("gx", "gy", "gz", None, None, None, None, None),
            P("gx", "gy", "gz", None, None, None, None),
        ),
        check_vma=False,
    )
```

```python
import functools

import jax
import jax.numpy as jnp
from jax import lax
from jax.experimental import pallas as pl
from jax.experimental.pallas import tpu as pltpu
from jax.sharding import PartitionSpec as P

NV = 32
POOL = 48
TB = 2
DOF = 12
HALF = DOF // 2
SITES = 256
RHS = 32
NC = 64
LANES = 2 * NC
ROWS = 16
UNITS = tuple((t, first) for t in range(TB) for first in range(0, RHS, ROWS))
SIDES = (
    ("gz", 1, 5),
    ("gz", -1, 6),
    ("gx", 1, 1),
    ("gx", -1, 2),
    ("gy", 1, 3),
    ("gy", -1, 4),
)
NEAR = (0, 1, 2, 3)
FAR = (4, 5)
NT = (((1,), (1,)), ((), ()))
NN = (((1,), (0,)), ((), ()))


def dot(a, b, dims):
    return lax.dot_general(a, b, dims, preferred_element_type=jnp.float32)


def step_on(axis, step, size):
    return lax.rem(lax.axis_index(axis) + (step + size), size)


def picked(pick, p, h):
    lane = lax.broadcasted_iota(jnp.int32, (2 * POOL, LANES), 1)
    row = lax.broadcasted_iota(jnp.int32, (2 * POOL, LANES), 0)
    wanted = jnp.concatenate([pick] * (LANES // NV), axis=1)
    part = row & 1
    hit = (row >> 1 == wanted) & (((lane >> 5) & 1) == h) & ((part ^ p) == lane >> 6)
    sign = jnp.where((part == 1) & (p == 0), -1.0, 1.0)
    return jnp.where(hit, sign, 0.0).astype(jnp.bfloat16)


def kernel(
    sizes,
    pick_ref,
    fine_ref,
    cand_ref,
    links_ref,
    err_ref,
    factor_ref,
    chosen_v,
    fine_v,
    cand_v,
    links_v,
    oper_v,
    rhs_v,
    mid_v,
    got_v,
    pick_v,
    in_sem,
    send_sem,
    recv_sem,
):
    barrier = pltpu.get_barrier_semaphore()
    for axis, step, _ in reversed(SIDES):
        pl.semaphore_signal(
            barrier,
            inc=1,
            device_id={axis: step_on(axis, step, sizes[axis])},
            device_id_type=pl.DeviceIdType.MESH,
        )

    loads = [pltpu.make_async_copy(pick_ref, pick_v, in_sem.at[5])]
    for t in range(TB):
        loads.append(pltpu.make_async_copy(cand_ref.at[t], cand_v.at[t], in_sem.at[2 * t]))
        loads.append(pltpu.make_async_copy(fine_ref.at[t], fine_v.at[t], in_sem.at[2 * t + 1]))
    loads.append(pltpu.make_async_copy(links_ref.at[lax.axis_index("gx")], links_v, in_sem.at[4]))

    for load in loads:
        load.start()

    def transfer(turn, unit, side):
        t, first = UNITS[unit]
        rows = pl.ds(first, ROWS)
        axis, step, _ = SIDES[side]
        return pltpu.make_async_remote_copy(
            src_ref=(rhs_v, mid_v)[turn].at[t, rows],
            dst_ref=got_v.at[turn, side, t, rows],
            send_sem=send_sem.at[turn, unit, side],
            recv_sem=recv_sem.at[turn, unit, side],
            device_id={axis: step_on(axis, -step, sizes[axis])},
            device_id_type=pl.DeviceIdType.MESH,
        )

    loads[0].wait()
    select = [[picked(pick_v[...], p, h) for h in range(2)] for p in range(2)]

    for t in range(TB):
        loads[2 * t + 1].wait()
        loads[2 * t + 2].wait()
        total = jnp.zeros((RHS, LANES), jnp.float32)
        for h in range(2):
            some = range(h * HALF, (h + 1) * HALF)
            for a in some:
                chosen_v[t, a] = cand_v[t, :, a].reshape(2 * POOL, SITES)
            vectors = jnp.concatenate([chosen_v[t, a] for a in some], axis=1)
            field = jnp.concatenate([fine_v[t, :, a].reshape(2 * RHS, SITES) for a in some], axis=1)
            terms = dot(field, vectors, NT)
            high = terms.astype(jnp.bfloat16)
            rest = terms - high.astype(jnp.float32)
            low = rest.astype(jnp.bfloat16)
            lowest = (rest - low.astype(jnp.float32)).astype(jnp.bfloat16)
            for p in range(2):
                here = slice(p * RHS, (p + 1) * RHS)
                for piece in (high, low, lowest):
                    total = total + dot(piece[here], select[p][h], NN)
        rhs_v[t] = total

    loads[5].wait()
    lane = lax.broadcasted_iota(jnp.int32, (NC, LANES), 1)
    for t in range(TB):
        blocks = [links_v[t, 0], -(links_v[t, 7] + links_v[t, 8])]
        blocks = blocks + [-links_v[t, link] for _, _, link in SIDES]
        for i, block in enumerate(blocks):
            signed = jnp.where(lane < NC, block, -block)
            turned = pltpu.roll(block, NC, 1)
            whole = jnp.concatenate([signed, turned], axis=0)
            oper_v[t, i * LANES : (i + 1) * LANES] = whole.T.astype(jnp.bfloat16)

    pl.semaphore_wait(barrier, len(SIDES))
    for unit in range(len(UNITS)):
        for side in FAR:
            transfer(0, unit, side).start()
        if unit:
            for side in NEAR:
                transfer(0, unit - 1, side).start()
    for side in NEAR:
        transfer(0, len(UNITS) - 1, side).start()

    def image(turn, unit):
        t, first = UNITS[unit]
        rows = pl.ds(first, ROWS)
        vector = (rhs_v, mid_v)[turn]
        total = jnp.zeros((ROWS, LANES), jnp.float32)
        parts = [vector[t, rows], vector[1 - t, rows]]
        column = 0
        for sides in (NEAR, FAR):
            for side in sides:
                transfer(turn, unit, side).wait_recv()
                parts.append(got_v[turn, side, t, rows])
            joined = jnp.concatenate([part.astype(jnp.bfloat16) for part in parts], axis=1)
            width = joined.shape[1]
            total = total + dot(joined, oper_v[t, column : column + width], NN)
            column = column + width
            parts = []
        return total

    for unit, (t, first) in enumerate(UNITS):
        rows = pl.ds(first, ROWS)
        mid_v[t, rows] = 0.75 * rhs_v[t, rows] - 0.25 * image(0, unit)
        for side in FAR + NEAR:
            transfer(1, unit, side).start()

    for unit, (t, first) in enumerate(UNITS):
        rows = pl.ds(first, ROWS)
        error = 0.5 * (mid_v[t, rows] + rhs_v[t, rows] - image(1, unit))
        err_ref[t, rows] = error
        error_half = error.astype(jnp.bfloat16)
        for h in range(2):
            for q in range(2):
                factor = dot(error_half, select[q][h], NT).astype(jnp.bfloat16)
                factor_ref[t, h, pl.ds(q * RHS + first, ROWS)] = factor

    for turn in range(2):
        for unit in range(len(UNITS)):
            for side in range(len(SIDES)):
                transfer(turn, unit, side).wait_send()


def prolong(error_ref, factor_ref, chosen_ref, corr_ref, err_ref, corr_v, err_v, sems):
    for t in range(TB):
        err_v[t, 0] = error_ref[t, :, :NC]
        err_v[t, 1] = error_ref[t, :, NC:]
    stores = [pltpu.make_async_copy(err_v, err_ref, sems.at[4])]
    stores[0].start()
    for t in range(TB):
        for h in range(2):
            for a in range(h * HALF, (h + 1) * HALF):
                out = dot(factor_ref[t, h], chosen_ref[t, a], NN).astype(jnp.bfloat16)
                corr_v[t, 0, a] = out[:RHS]
                corr_v[t, 1, a] = out[RHS:]
            some = pl.ds(h * HALF, HALF)
            store = pltpu.make_async_copy(
                corr_v.at[t, :, some], corr_ref.at[t, :, some], sems.at[2 * t + h]
            )
            store.start()
            stores.append(store)
    for store in stores:
        store.wait()


def on_device(sizes, fine_residual, candidates, vector_pick, coarse_links):
    fine = fine_residual[0, 0, 0]
    pool = jnp.swapaxes(candidates[0, 0, 0], 2, 3)
    links = coarse_links[:, 0, 0]
    hbm = pl.BlockSpec(memory_space=pltpu.HBM)
    sides = len(SIDES)
    error, factor, chosen = pl.pallas_call(
        functools.partial(kernel, sizes),
        out_shape=(
            pltpu.VMEM((TB, RHS, LANES), jnp.float32),
            pltpu.VMEM((TB, 2, 2 * RHS, 2 * POOL), jnp.bfloat16),
            pltpu.VMEM((TB, DOF, 2 * POOL, SITES), jnp.bfloat16),
        ),
        in_specs=[hbm] * 4,
        out_specs=(pl.BlockSpec(memory_space=pltpu.VMEM),) * 3,
        scratch_shapes=[
            pltpu.VMEM((TB, 2, DOF, RHS, SITES), jnp.bfloat16),
            pltpu.VMEM((TB, POOL, DOF, 2, SITES), jnp.bfloat16),
            pltpu.VMEM((TB, 9, NC, LANES), jnp.float32),
            pltpu.VMEM((TB, 8 * LANES, LANES), jnp.bfloat16),
            pltpu.VMEM((TB, RHS, LANES), jnp.float32),
            pltpu.VMEM((TB, RHS, LANES), jnp.float32),
            pltpu.VMEM((2, sides, TB, RHS, LANES), jnp.float32),
            pltpu.VMEM((1, NV), jnp.int32),
            pltpu.SemaphoreType.DMA((6,)),
            pltpu.SemaphoreType.DMA((2, len(UNITS), sides)),
            pltpu.SemaphoreType.DMA((2, len(UNITS), sides)),
        ],
        compiler_params=pltpu.CompilerParams(
            collective_id=0, has_side_effects=True, vmem_limit_bytes=48 << 20
        ),
        name="coarse_correction",
    )(*[pltpu.with_memory_space_constraint(x, pltpu.HBM) for x in (vector_pick[None], fine, pool, links)])
    vmem = pl.BlockSpec(memory_space=pltpu.VMEM)
    correction, error = pl.pallas_call(
        prolong,
        out_shape=(
            pltpu.HBM((TB, 2, DOF, RHS, SITES), jnp.bfloat16),
            pltpu.HBM((TB, 2, RHS, NC), jnp.float32),
        ),
        in_specs=[vmem] * 3,
        out_specs=(hbm, hbm),
        scratch_shapes=[
            pltpu.VMEM((TB, 2, DOF, RHS, SITES), jnp.bfloat16),
            pltpu.VMEM((TB, 2, RHS, NC), jnp.float32),
            pltpu.SemaphoreType.DMA((5,)),
        ],
        compiler_params=pltpu.CompilerParams(vmem_limit_bytes=32 << 20),
        name="prolong",
    )(*[pltpu.with_memory_space_constraint(x, pltpu.VMEM) for x in (error, factor, chosen)])
    return (correction[None, None, None], jnp.swapaxes(error, 2, 3)[None, None, None])


def solution(mesh):
    placed = (
        P("gx", "gy", "gz", None, None, None, None, None),
        P("gx", "gy", "gz", None, None, None, None, None),
        P(),
        P(None, "gy", "gz", None, None, None, None),
    )
    return jax.shard_map(
        functools.partial(on_device, dict(mesh.shape)),
        mesh=mesh,
        in_specs=placed,
        out_specs=(
            P("gx", "gy", "gz", None, None, None, None, None),
            P("gx", "gy", "gz", None, None, None, None),
        ),
        check_vma=False,
    )
```

```python
import functools

import jax
import jax.numpy as jnp
from jax import lax
from jax.experimental import pallas as pl
from jax.experimental.pallas import tpu as pltpu
from jax.sharding import PartitionSpec as P

NV = 32
POOL = 48
TB = 2
DOF = 12
HALF = DOF // 2
SITES = 256
RHS = 32
NC = 64
LANES = 2 * NC
ROWS = 16
UNITS = tuple((t, first) for t in range(TB) for first in range(0, RHS, ROWS))
SIDES = (
    ("gz", 1, 5),
    ("gz", -1, 6),
    ("gx", 1, 1),
    ("gx", -1, 2),
    ("gy", 1, 3),
    ("gy", -1, 4),
)
LAST = len(UNITS) - 1
NEAR = (0, 1, 2, 3)
FAR = (4, 5)
NT = (((1,), (1,)), ((), ()))
NN = (((1,), (0,)), ((), ()))


def dot(a, b, dims):
    return lax.dot_general(a, b, dims, preferred_element_type=jnp.float32)


def step_on(axis, step, size):
    return lax.rem(lax.axis_index(axis) + (step + size), size)


def picked(pick, p, h):
    lane = lax.broadcasted_iota(jnp.int32, (LANES, LANES), 1)
    row = lax.broadcasted_iota(jnp.int32, (LANES, LANES), 0)
    wanted = jnp.concatenate([pick] * (LANES // NV), axis=1)
    part = row & 1
    hit = (row >> 1 == wanted) & (((lane >> 5) & 1) == h) & ((part ^ p) == lane >> 6)
    sign = jnp.where((part == 1) & (p == 0), -1.0, 1.0)
    return jnp.where(hit, sign, 0.0)


def kernel(
    sizes,
    pick_ref,
    fine_ref,
    cand_ref,
    links_ref,
    err_ref,
    factor_ref,
    chosen_v,
    fine_v,
    cand_v,
    links_v,
    oper_v,
    oper_low_v,
    rhs_v,
    mid_v,
    got_v,
    pick_v,
    select_v,
    spread_v,
    in_sem,
    send_sem,
    recv_sem,
):
    barrier = pltpu.get_barrier_semaphore()
    for axis, step, _ in reversed(SIDES):
        pl.semaphore_signal(
            barrier,
            inc=1,
            device_id={axis: step_on(axis, step, sizes[axis])},
            device_id_type=pl.DeviceIdType.MESH,
        )

    loads = [pltpu.make_async_copy(pick_ref, pick_v, in_sem.at[5])]
    for t in range(TB):
        loads.append(pltpu.make_async_copy(cand_ref.at[t], cand_v.at[t], in_sem.at[2 * t]))
        loads.append(pltpu.make_async_copy(fine_ref.at[t], fine_v.at[t], in_sem.at[2 * t + 1]))
    loads.append(pltpu.make_async_copy(links_ref.at[lax.axis_index("gx")], links_v, in_sem.at[4]))

    for load in loads:
        load.start()

    def transfer(turn, unit, side):
        t, first = UNITS[unit]
        rows = pl.ds(first, ROWS)
        axis, step, _ = SIDES[side]
        return pltpu.make_async_remote_copy(
            src_ref=(rhs_v, mid_v)[turn].at[t, rows],
            dst_ref=got_v.at[turn, side, t, rows],
            send_sem=send_sem.at[turn, unit, side],
            recv_sem=recv_sem.at[turn, unit, side],
            device_id={axis: step_on(axis, -step, sizes[axis])},
            device_id_type=pl.DeviceIdType.MESH,
        )

    loads[0].wait()
    for p in range(2):
        for h in range(2):
            matrix = picked(pick_v[...], p, h)
            select_v[p, h] = matrix[: 2 * POOL].astype(jnp.bfloat16)
            columns = slice((2 * p + h) * LANES, (2 * p + h + 1) * LANES)
            spread_v[:, columns] = matrix.T.astype(jnp.bfloat16)

    def restrict(t):
        loads[2 * t + 1].wait()
        loads[2 * t + 2].wait()
        total = jnp.zeros((RHS, LANES), jnp.float32)
        for h in range(2):
            some = range(h * HALF, (h + 1) * HALF)
            for a in some:
                chosen_v[t, a] = cand_v[t, :, a].reshape(2 * POOL, SITES)
            vectors = jnp.concatenate([chosen_v[t, a] for a in some], axis=1)
            field = jnp.concatenate([fine_v[t, :, a].reshape(2 * RHS, SITES) for a in some], axis=1)
            terms = dot(field, vectors, NT)
            high = terms.astype(jnp.bfloat16)
            rest = terms - high.astype(jnp.float32)
            low = rest.astype(jnp.bfloat16)
            lowest = (rest - low.astype(jnp.float32)).astype(jnp.bfloat16)
            for p in range(2):
                here = slice(p * RHS, (p + 1) * RHS)
                for piece in (high, low, lowest):
                    total = total + dot(piece[here], select_v[p, h], NN)
        rhs_v[t] = total

    lane = lax.broadcasted_iota(jnp.int32, (NC, LANES), 1)

    def build(t):
        blocks = [links_v[t, 0], -(links_v[t, 7] + links_v[t, 8])]
        blocks = blocks + [-links_v[t, link] for _, _, link in SIDES]
        for i, block in enumerate(blocks):
            signed = jnp.where(lane < NC, block, -block)
            turned = pltpu.roll(block, NC, 1)
            whole = jnp.concatenate([signed, turned], axis=0)
            whole = whole.T
            high = whole.astype(jnp.bfloat16)
            rows = slice(i * LANES, (i + 1) * LANES)
            oper_v[t, rows] = high
            oper_low_v[t, rows] = (whole - high.astype(jnp.float32)).astype(jnp.bfloat16)

    def begin(turn, unit):
        for side in FAR + NEAR:
            transfer(turn, unit, side).start()

    restrict(0)
    pl.semaphore_wait(barrier, len(SIDES))
    begin(0, 0)
    loads[5].wait()
    build(0)
    begin(0, 1)
    restrict(1)
    begin(0, 2)
    build(1)
    begin(0, 3)

    def image(turn, unit):
        t, first = UNITS[unit]
        rows = pl.ds(first, ROWS)
        vector = (rhs_v, mid_v)[turn]
        total = jnp.zeros((ROWS, LANES), jnp.float32)
        parts = [vector[t, rows], vector[1 - t, rows]]
        column = 0
        for sides in (NEAR, FAR):
            for side in sides:
                transfer(turn, unit, side).wait_recv()
                parts.append(got_v[turn, side, t, rows])
            joined = jnp.concatenate(parts, axis=1)
            high = joined.astype(jnp.bfloat16)
            low = (joined - high.astype(jnp.float32)).astype(jnp.bfloat16)
            width = joined.shape[1]
            both = dot(jnp.concatenate([high, low], axis=0), oper_v[t, column : column + width], NN)
            rest = dot(high, oper_low_v[t, column : column + width], NN)
            total = total + (both[:ROWS] + both[ROWS:] + rest)
            column = column + width
            parts = []
        return total

    for unit, (t, first) in enumerate(UNITS):
        rows = pl.ds(first, ROWS)
        mid_v[t, rows] = 0.75 * rhs_v[t, rows] - 0.25 * image(0, unit)
        begin(1, unit)

    for unit, (t, first) in enumerate(UNITS):
        rows = pl.ds(first, ROWS)
        if unit == LAST:
            for turn in range(2):
                for sent in range(len(UNITS)):
                    for side in range(len(SIDES)):
                        transfer(turn, sent, side).wait_send()
        error = 0.5 * (mid_v[t, rows] + rhs_v[t, rows] - image(1, unit))
        err_ref[t, rows] = error
        factors = dot(error.astype(jnp.bfloat16), spread_v[...], NN).astype(jnp.bfloat16)
        for h in range(2):
            for q in range(2):
                column = (2 * q + h) * LANES
                factor_ref[t, h, pl.ds(q * RHS + first, ROWS)] = factors[:, column : column + 2 * POOL]


def prolong(error_ref, factor_ref, chosen_ref, corr_ref, err_ref, corr_v, err_v, sems):
    for t in range(TB):
        err_v[t, 0] = error_ref[t, :, :NC]
        err_v[t, 1] = error_ref[t, :, NC:]
    stores = [pltpu.make_async_copy(err_v, err_ref, sems.at[4])]
    stores[0].start()
    for t in range(TB):
        for h in range(2):
            for a in range(h * HALF, (h + 1) * HALF):
                out = dot(factor_ref[t, h], chosen_ref[t, a], NN).astype(jnp.bfloat16)
                corr_v[t, 0, a] = out[:RHS]
                corr_v[t, 1, a] = out[RHS:]
            some = pl.ds(h * HALF, HALF)
            store = pltpu.make_async_copy(
                corr_v.at[t, :, some], corr_ref.at[t, :, some], sems.at[2 * t + h]
            )
            store.start()
            stores.append(store)
    for store in stores:
        store.wait()


def on_device(sizes, fine_residual, candidates, vector_pick, coarse_links):
    fine = fine_residual[0, 0, 0]
    pool = jnp.swapaxes(candidates[0, 0, 0], 2, 3)
    links = coarse_links[:, 0, 0]
    hbm = pl.BlockSpec(memory_space=pltpu.HBM)
    sides = len(SIDES)
    error, factor, chosen = pl.pallas_call(
        functools.partial(kernel, sizes),
        out_shape=(
            pltpu.VMEM((TB, RHS, LANES), jnp.float32),
            pltpu.VMEM((TB, 2, 2 * RHS, 2 * POOL), jnp.bfloat16),
            pltpu.VMEM((TB, DOF, 2 * POOL, SITES), jnp.bfloat16),
        ),
        in_specs=[hbm] * 4,
        out_specs=(pl.BlockSpec(memory_space=pltpu.VMEM),) * 3,
        scratch_shapes=[
            pltpu.VMEM((TB, 2, DOF, RHS, SITES), jnp.bfloat16),
            pltpu.VMEM((TB, POOL, DOF, 2, SITES), jnp.bfloat16),
            pltpu.VMEM((TB, 9, NC, LANES), jnp.float32),
            pltpu.VMEM((TB, 8 * LANES, LANES), jnp.bfloat16),
            pltpu.VMEM((TB, 8 * LANES, LANES), jnp.bfloat16),
            pltpu.VMEM((TB, RHS, LANES), jnp.float32),
            pltpu.VMEM((TB, RHS, LANES), jnp.float32),
            pltpu.VMEM((2, sides, TB, RHS, LANES), jnp.float32),
            pltpu.VMEM((1, NV), jnp.int32),
            pltpu.VMEM((2, 2, 2 * POOL, LANES), jnp.bfloat16),
            pltpu.VMEM((LANES, 4 * LANES), jnp.bfloat16),
            pltpu.SemaphoreType.DMA((6,)),
            pltpu.SemaphoreType.DMA((2, len(UNITS), sides)),
            pltpu.SemaphoreType.DMA((2, len(UNITS), sides)),
        ],
        compiler_params=pltpu.CompilerParams(
            collective_id=0, has_side_effects=True, vmem_limit_bytes=48 << 20
        ),
        name="coarse_correction",
    )(*[pltpu.with_memory_space_constraint(x, pltpu.HBM) for x in (vector_pick[None], fine, pool, links)])
    vmem = pl.BlockSpec(memory_space=pltpu.VMEM)
    correction, error = pl.pallas_call(
        prolong,
        out_shape=(
            pltpu.HBM((TB, 2, DOF, RHS, SITES), jnp.bfloat16),
            pltpu.HBM((TB, 2, RHS, NC), jnp.float32),
        ),
        in_specs=[vmem] * 3,
        out_specs=(hbm, hbm),
        scratch_shapes=[
            pltpu.VMEM((TB, 2, DOF, RHS, SITES), jnp.bfloat16),
            pltpu.VMEM((TB, 2, RHS, NC), jnp.float32),
            pltpu.SemaphoreType.DMA((5,)),
        ],
        compiler_params=pltpu.CompilerParams(vmem_limit_bytes=32 << 20),
        name="prolong",
    )(*[pltpu.with_memory_space_constraint(x, pltpu.VMEM) for x in (error, factor, chosen)])
    return (correction[None, None, None], jnp.swapaxes(error, 2, 3)[None, None, None])


def solution(mesh):
    placed = (
        P("gx", "gy", "gz", None, None, None, None, None),
        P("gx", "gy", "gz", None, None, None, None, None),
        P(),
        P(None, "gy", "gz", None, None, None, None),
    )
    return jax.shard_map(
        functools.partial(on_device, dict(mesh.shape)),
        mesh=mesh,
        in_specs=placed,
        out_specs=(
            P("gx", "gy", "gz", None, None, None, None, None),
            P("gx", "gy", "gz", None, None, None, None),
        ),
        check_vma=False,
    )
```

```python
import functools

import jax
import jax.numpy as jnp
from jax import lax
from jax.experimental import pallas as pl
from jax.experimental.pallas import tpu as pltpu
from jax.sharding import PartitionSpec as P

NV = 32
POOL = 48
TB = 2
DOF = 12
HALF = DOF // 2
SITES = 256
RHS = 32
NC = 64
LANES = 2 * NC
ROWS = 16
UNITS = tuple((t, first) for t in range(TB) for first in range(0, RHS, ROWS))
SIDES = (
    ("gz", 1, 5),
    ("gz", -1, 6),
    ("gx", 1, 1),
    ("gx", -1, 2),
    ("gy", 1, 3),
    ("gy", -1, 4),
)
LAST = len(UNITS) - 1
NEAR = (0, 1, 2, 3)
FAR = (4, 5)
NT = (((1,), (1,)), ((), ()))
NN = (((1,), (0,)), ((), ()))


def dot(a, b, dims):
    return lax.dot_general(a, b, dims, preferred_element_type=jnp.float32)


def step_on(axis, step, size):
    return lax.rem(lax.axis_index(axis) + (step + size), size)


def picked(pick, p, h):
    lane = lax.broadcasted_iota(jnp.int32, (LANES, LANES), 1)
    row = lax.broadcasted_iota(jnp.int32, (LANES, LANES), 0)
    wanted = jnp.concatenate([pick] * (LANES // NV), axis=1)
    part = row & 1
    hit = (row >> 1 == wanted) & (((lane >> 5) & 1) == h) & ((part ^ p) == lane >> 6)
    sign = jnp.where((part == 1) & (p == 0), -1.0, 1.0)
    return jnp.where(hit, sign, 0.0)


def kernel(
    sizes,
    pick_ref,
    fine_ref,
    cand_ref,
    links_ref,
    err_ref,
    factor_ref,
    chosen_v,
    fine_v,
    cand_v,
    links_v,
    oper_v,
    rhs_v,
    mid_v,
    got_v,
    pick_v,
    select_v,
    spread_v,
    in_sem,
    send_sem,
    recv_sem,
):
    barrier = pltpu.get_barrier_semaphore()
    for axis, step, _ in reversed(SIDES):
        pl.semaphore_signal(
            barrier,
            inc=1,
            device_id={axis: step_on(axis, step, sizes[axis])},
            device_id_type=pl.DeviceIdType.MESH,
        )

    loads = [pltpu.make_async_copy(pick_ref, pick_v, in_sem.at[5])]
    for t in range(TB):
        loads.append(pltpu.make_async_copy(cand_ref.at[t], cand_v.at[t], in_sem.at[2 * t]))
        loads.append(pltpu.make_async_copy(fine_ref.at[t], fine_v.at[t], in_sem.at[2 * t + 1]))
    loads.append(pltpu.make_async_copy(links_ref.at[lax.axis_index("gx")], links_v, in_sem.at[4]))

    for load in loads:
        load.start()

    def transfer(turn, unit, side):
        t, first = UNITS[unit]
        rows = pl.ds(first, ROWS)
        axis, step, _ = SIDES[side]
        return pltpu.make_async_remote_copy(
            src_ref=(rhs_v, mid_v)[turn].at[t, rows],
            dst_ref=got_v.at[turn, side, t, rows],
            send_sem=send_sem.at[turn, unit, side],
            recv_sem=recv_sem.at[turn, unit, side],
            device_id={axis: step_on(axis, -step, sizes[axis])},
            device_id_type=pl.DeviceIdType.MESH,
        )

    loads[0].wait()
    for p in range(2):
        for h in range(2):
            matrix = picked(pick_v[...], p, h)
            select_v[p, h] = matrix[: 2 * POOL].astype(jnp.bfloat16)
            columns = slice((2 * p + h) * LANES, (2 * p + h + 1) * LANES)
            spread_v[:, columns] = matrix.T.astype(jnp.bfloat16)

    def restrict(t):
        loads[2 * t + 1].wait()
        loads[2 * t + 2].wait()
        total = jnp.zeros((RHS, LANES), jnp.float32)
        for h in range(2):
            some = range(h * HALF, (h + 1) * HALF)
            for a in some:
                chosen_v[t, a] = cand_v[t, :, a].reshape(2 * POOL, SITES)
            vectors = jnp.concatenate([chosen_v[t, a] for a in some], axis=1)
            field = jnp.concatenate([fine_v[t, :, a].reshape(2 * RHS, SITES) for a in some], axis=1)
            terms = dot(field, vectors, NT)
            high = terms.astype(jnp.bfloat16)
            rest = terms - high.astype(jnp.float32)
            low = rest.astype(jnp.bfloat16)
            lowest = (rest - low.astype(jnp.float32)).astype(jnp.bfloat16)
            for p in range(2):
                here = slice(p * RHS, (p + 1) * RHS)
                for piece in (high, low, lowest):
                    total = total + dot(piece[here], select_v[p, h], NN)
        rhs_v[t] = total

    lane = lax.broadcasted_iota(jnp.int32, (NC, LANES), 1)

    def build(t):
        blocks = [links_v[t, 0], -(links_v[t, 7] + links_v[t, 8])]
        blocks = blocks + [-links_v[t, link] for _, _, link in SIDES]
        for i, block in enumerate(blocks):
            signed = jnp.where(lane < NC, block, -block)
            turned = pltpu.roll(block, NC, 1)
            whole = jnp.concatenate([signed, turned], axis=0)
            oper_v[t, i * LANES : (i + 1) * LANES] = whole.T.astype(jnp.bfloat16)

    def begin(turn, unit):
        for side in FAR + NEAR:
            transfer(turn, unit, side).start()

    restrict(0)
    pl.semaphore_wait(barrier, len(SIDES))
    begin(0, 0)
    loads[5].wait()
    build(0)
    begin(0, 1)
    restrict(1)
    begin(0, 2)
    build(1)
    begin(0, 3)

    def image(turn, unit):
        t, first = UNITS[unit]
        rows = pl.ds(first, ROWS)
        vector = (rhs_v, mid_v)[turn]
        total = jnp.zeros((ROWS, LANES), jnp.float32)
        parts = [vector[t, rows], vector[1 - t, rows]]
        column = 0
        for sides in (NEAR, FAR):
            for side in sides:
                transfer(turn, unit, side).wait_recv()
                parts.append(got_v[turn, side, t, rows])
            joined = jnp.concatenate([part.astype(jnp.bfloat16) for part in parts], axis=1)
            width = joined.shape[1]
            total = total + dot(joined, oper_v[t, column : column + width], NN)
            column = column + width
            parts = []
        return total

    for unit, (t, first) in enumerate(UNITS):
        rows = pl.ds(first, ROWS)
        mid_v[t, rows] = 0.75 * rhs_v[t, rows] - 0.25 * image(0, unit)
        begin(1, unit)

    for unit, (t, first) in enumerate(UNITS):
        rows = pl.ds(first, ROWS)
        if unit == LAST:
            for turn in range(2):
                for sent in range(len(UNITS)):
                    for side in range(len(SIDES)):
                        transfer(turn, sent, side).wait_send()
        error = 0.5 * (mid_v[t, rows] + rhs_v[t, rows] - image(1, unit))
        err_ref[t, rows] = error
        factors = dot(error.astype(jnp.bfloat16), spread_v[...], NN).astype(jnp.bfloat16)
        for h in range(2):
            for q in range(2):
                column = (2 * q + h) * LANES
                factor_ref[t, h, pl.ds(q * RHS + first, ROWS)] = factors[:, column : column + 2 * POOL]


def prolong(error_ref, factor_ref, chosen_ref, corr_ref, err_ref, corr_v, err_v, sems):
    for t in range(TB):
        err_v[t, 0] = error_ref[t, :, :NC]
        err_v[t, 1] = error_ref[t, :, NC:]
    stores = [pltpu.make_async_copy(err_v, err_ref, sems.at[4])]
    stores[0].start()
    for t in range(TB):
        for h in range(2):
            for a in range(h * HALF, (h + 1) * HALF):
                out = dot(factor_ref[t, h], chosen_ref[t, a], NN).astype(jnp.bfloat16)
                corr_v[t, 0, a] = out[:RHS]
                corr_v[t, 1, a] = out[RHS:]
            some = pl.ds(h * HALF, HALF)
            store = pltpu.make_async_copy(
                corr_v.at[t, :, some], corr_ref.at[t, :, some], sems.at[2 * t + h]
            )
            store.start()
            stores.append(store)
    for store in stores:
        store.wait()


def on_device(sizes, fine_residual, candidates, vector_pick, coarse_links):
    fine = fine_residual[0, 0, 0]
    pool = jnp.swapaxes(candidates[0, 0, 0], 2, 3)
    links = coarse_links[:, 0, 0]
    hbm = pl.BlockSpec(memory_space=pltpu.HBM)
    sides = len(SIDES)
    error, factor, chosen = pl.pallas_call(
        functools.partial(kernel, sizes),
        out_shape=(
            pltpu.VMEM((TB, RHS, LANES), jnp.float32),
            pltpu.VMEM((TB, 2, 2 * RHS, 2 * POOL), jnp.bfloat16),
            pltpu.VMEM((TB, DOF, 2 * POOL, SITES), jnp.bfloat16),
        ),
        in_specs=[hbm] * 4,
        out_specs=(pl.BlockSpec(memory_space=pltpu.VMEM),) * 3,
        scratch_shapes=[
            pltpu.VMEM((TB, 2, DOF, RHS, SITES), jnp.bfloat16),
            pltpu.VMEM((TB, POOL, DOF, 2, SITES), jnp.bfloat16),
            pltpu.VMEM((TB, 9, NC, LANES), jnp.float32),
            pltpu.VMEM((TB, 8 * LANES, LANES), jnp.bfloat16),
            pltpu.VMEM((TB, RHS, LANES), jnp.float32),
            pltpu.VMEM((TB, RHS, LANES), jnp.float32),
            pltpu.VMEM((2, sides, TB, RHS, LANES), jnp.float32),
            pltpu.VMEM((1, NV), jnp.int32),
            pltpu.VMEM((2, 2, 2 * POOL, LANES), jnp.bfloat16),
            pltpu.VMEM((LANES, 4 * LANES), jnp.bfloat16),
            pltpu.SemaphoreType.DMA((6,)),
            pltpu.SemaphoreType.DMA((2, len(UNITS), sides)),
            pltpu.SemaphoreType.DMA((2, len(UNITS), sides)),
        ],
        compiler_params=pltpu.CompilerParams(
            collective_id=0, has_side_effects=True, vmem_limit_bytes=48 << 20
        ),
        name="coarse_correction",
    )(*[pltpu.with_memory_space_constraint(x, pltpu.HBM) for x in (vector_pick[None], fine, pool, links)])
    vmem = pl.BlockSpec(memory_space=pltpu.VMEM)
    correction, error = pl.pallas_call(
        prolong,
        out_shape=(
            pltpu.HBM((TB, 2, DOF, RHS, SITES), jnp.bfloat16),
            pltpu.HBM((TB, 2, RHS, NC), jnp.float32),
        ),
        in_specs=[vmem] * 3,
        out_specs=(hbm, hbm),
        scratch_shapes=[
            pltpu.VMEM((TB, 2, DOF, RHS, SITES), jnp.bfloat16),
            pltpu.VMEM((TB, 2, RHS, NC), jnp.float32),
            pltpu.SemaphoreType.DMA((5,)),
        ],
        compiler_params=pltpu.CompilerParams(vmem_limit_bytes=32 << 20),
        name="prolong",
    )(*[pltpu.with_memory_space_constraint(x, pltpu.VMEM) for x in (error, factor, chosen)])
    return (correction[None, None, None], jnp.swapaxes(error, 2, 3)[None, None, None])


def solution(mesh):
    placed = (
        P("gx", "gy", "gz", None, None, None, None, None),
        P("gx", "gy", "gz", None, None, None, None, None),
        P(),
        P(None, "gy", "gz", None, None, None, None),
    )
    return jax.shard_map(
        functools.partial(on_device, dict(mesh.shape)),
        mesh=mesh,
        in_specs=placed,
        out_specs=(
            P("gx", "gy", "gz", None, None, None, None, None),
            P("gx", "gy", "gz", None, None, None, None),
        ),
        check_vma=False,
    )
```

```python
import functools

import jax
import jax.numpy as jnp
from jax import lax
from jax.experimental import pallas as pl
from jax.experimental.pallas import tpu as pltpu
from jax.sharding import PartitionSpec as P

NV = 32
POOL = 48
TB = 2
DOF = 12
HALF = DOF // 2
SITES = 256
RHS = 32
NC = 64
LANES = 2 * NC
ROWS = 16
UNITS = tuple((t, first) for t in range(TB) for first in range(0, RHS, ROWS))
SIDES = (
    ("gz", 1, 5),
    ("gz", -1, 6),
    ("gx", 1, 1),
    ("gx", -1, 2),
    ("gy", 1, 3),
    ("gy", -1, 4),
)
LAST = len(UNITS) - 1
NEAR = (0, 1, 2, 3)
FAR = (4, 5)
NT = (((1,), (1,)), ((), ()))
NN = (((1,), (0,)), ((), ()))


def dot(a, b, dims):
    return lax.dot_general(a, b, dims, preferred_element_type=jnp.float32)


def step_on(axis, step, size):
    return lax.rem(lax.axis_index(axis) + (step + size), size)


def picked(pick, p, h):
    lane = lax.broadcasted_iota(jnp.int32, (LANES, LANES), 1)
    row = lax.broadcasted_iota(jnp.int32, (LANES, LANES), 0)
    wanted = jnp.concatenate([pick] * (LANES // NV), axis=1)
    part = row & 1
    hit = (row >> 1 == wanted) & (((lane >> 5) & 1) == h) & ((part ^ p) == lane >> 6)
    sign = jnp.where((part == 1) & (p == 0), -1.0, 1.0)
    return jnp.where(hit, sign, 0.0)


def kernel(
    sizes,
    pick_ref,
    fine_ref,
    cand_ref,
    links_ref,
    err_ref,
    factor_ref,
    chosen_v,
    fine_v,
    cand_v,
    links_v,
    oper_v,
    oper_low_v,
    rhs_v,
    mid_v,
    got_v,
    pick_v,
    select_v,
    spread_v,
    in_sem,
    send_sem,
    recv_sem,
):
    barrier = pltpu.get_barrier_semaphore()
    for axis, step, _ in reversed(SIDES):
        pl.semaphore_signal(
            barrier,
            inc=1,
            device_id={axis: step_on(axis, step, sizes[axis])},
            device_id_type=pl.DeviceIdType.MESH,
        )

    loads = [pltpu.make_async_copy(pick_ref, pick_v, in_sem.at[5])]
    for t in range(TB):
        loads.append(pltpu.make_async_copy(cand_ref.at[t], cand_v.at[t], in_sem.at[2 * t]))
        loads.append(pltpu.make_async_copy(fine_ref.at[t], fine_v.at[t], in_sem.at[2 * t + 1]))
    loads.append(pltpu.make_async_copy(links_ref.at[lax.axis_index("gx")], links_v, in_sem.at[4]))

    for load in loads:
        load.start()

    def transfer(turn, unit, side):
        t, first = UNITS[unit]
        rows = pl.ds(first, ROWS)
        axis, step, _ = SIDES[side]
        return pltpu.make_async_remote_copy(
            src_ref=(rhs_v, mid_v)[turn].at[t, rows],
            dst_ref=got_v.at[turn, side, t, rows],
            send_sem=send_sem.at[turn, unit, side],
            recv_sem=recv_sem.at[turn, unit, side],
            device_id={axis: step_on(axis, -step, sizes[axis])},
            device_id_type=pl.DeviceIdType.MESH,
        )

    loads[0].wait()
    for p in range(2):
        for h in range(2):
            matrix = picked(pick_v[...], p, h)
            select_v[p, h] = matrix[: 2 * POOL].astype(jnp.bfloat16)
            columns = slice((2 * p + h) * LANES, (2 * p + h + 1) * LANES)
            spread_v[:, columns] = matrix.T.astype(jnp.bfloat16)

    def restrict(t):
        loads[2 * t + 1].wait()
        loads[2 * t + 2].wait()
        total = jnp.zeros((RHS, LANES), jnp.float32)
        for h in range(2):
            some = range(h * HALF, (h + 1) * HALF)
            for a in some:
                chosen_v[t, a] = cand_v[t, :, a].reshape(2 * POOL, SITES)
            vectors = jnp.concatenate([chosen_v[t, a] for a in some], axis=1)
            field = jnp.concatenate([fine_v[t, :, a].reshape(2 * RHS, SITES) for a in some], axis=1)
            terms = dot(field, vectors, NT)
            high = terms.astype(jnp.bfloat16)
            rest = terms - high.astype(jnp.float32)
            low = rest.astype(jnp.bfloat16)
            lowest = (rest - low.astype(jnp.float32)).astype(jnp.bfloat16)
            for p in range(2):
                here = slice(p * RHS, (p + 1) * RHS)
                for piece in (high, low, lowest):
                    total = total + dot(piece[here], select_v[p, h], NN)
        rhs_v[t] = total

    lane = lax.broadcasted_iota(jnp.int32, (NC, LANES), 1)

    def build(t):
        blocks = [links_v[t, 0], -(links_v[t, 7] + links_v[t, 8])]
        blocks = blocks + [-links_v[t, link] for _, _, link in SIDES]
        for i, block in enumerate(blocks):
            signed = jnp.where(lane < NC, block, -block)
            turned = pltpu.roll(block, NC, 1)
            whole = jnp.concatenate([signed, turned], axis=0)
            whole = whole.T
            high = whole.astype(jnp.bfloat16)
            rows = slice(i * LANES, (i + 1) * LANES)
            oper_v[t, rows] = high
            oper_low_v[t, rows] = (whole - high.astype(jnp.float32)).astype(jnp.bfloat16)

    part = lax.rem(lax.axis_index("gy"), 4)

    def urgent(turn, side):
        if turn == 0:
            return (part != 2, part != 2, part != 2, part != 2, part != 3, part != 4)[side]
        return (part == 0, part == 0, part == 0, part == 0, part == 1, part == 3)[side]

    def begin(turn, unit, now=True):
        for side in FAR[::-1] + NEAR:

            @pl.when(urgent(turn, side) if now else jnp.logical_not(urgent(turn, side)))
            def _():
                transfer(turn, unit, side).start()

    restrict(0)
    pl.semaphore_wait(barrier, len(SIDES))
    begin(0, 0)
    loads[5].wait()
    build(0)
    begin(0, 1)
    restrict(1)
    begin(0, 2)
    build(1)
    begin(0, 3)
    for unit in range(len(UNITS)):
        begin(0, unit, now=False)

    def gathered(turn, unit, parts, sides, column):
        t, first = UNITS[unit]
        rows = pl.ds(first, ROWS)
        for side in sides:
            transfer(turn, unit, side).wait_recv()
            parts = parts + [got_v[turn, side, t, rows]]
        joined = jnp.concatenate(parts, axis=1)
        high = joined.astype(jnp.bfloat16)
        low = (joined - high.astype(jnp.float32)).astype(jnp.bfloat16)
        here = slice(column, column + joined.shape[1])
        both = dot(jnp.concatenate([high, low], axis=0), oper_v[t, here], NN)
        return both[:ROWS] + both[ROWS:] + dot(high, oper_low_v[t, here], NN)

    def near(turn, unit):
        t, first = UNITS[unit]
        rows = pl.ds(first, ROWS)
        vector = (rhs_v, mid_v)[turn]
        return gathered(turn, unit, [vector[t, rows], vector[1 - t, rows]], NEAR, 0)

    def far(turn, unit):
        return gathered(turn, unit, [], FAR, (2 + len(NEAR)) * LANES)

    ahead = near(0, 0)
    for unit, (t, first) in enumerate(UNITS):
        rows = pl.ds(first, ROWS)
        image = ahead
        if unit < LAST:
            ahead = near(0, unit + 1)
        image = image + far(0, unit)
        mid_v[t, rows] = 0.75 * rhs_v[t, rows] - 0.25 * image
        begin(1, unit)
    for unit in range(len(UNITS)):
        begin(1, unit, now=False)

    ahead = near(1, 0)
    for unit, (t, first) in enumerate(UNITS):
        rows = pl.ds(first, ROWS)
        image = ahead
        if unit < LAST:
            ahead = near(1, unit + 1)
        else:
            for turn in range(2):
                for sent in range(len(UNITS)):
                    for side in range(len(SIDES)):
                        transfer(turn, sent, side).wait_send()
        image = image + far(1, unit)
        error = 0.5 * (mid_v[t, rows] + rhs_v[t, rows] - image)
        err_ref[t, rows] = error
        factors = dot(error.astype(jnp.bfloat16), spread_v[...], NN).astype(jnp.bfloat16)
        for h in range(2):
            for q in range(2):
                column = (2 * q + h) * LANES
                factor_ref[t, h, pl.ds(q * RHS + first, ROWS)] = factors[:, column : column + 2 * POOL]


def prolong(error_ref, factor_ref, chosen_ref, corr_ref, err_ref, corr_v, err_v, sems):
    for t in range(TB):
        err_v[t, 0] = error_ref[t, :, :NC]
        err_v[t, 1] = error_ref[t, :, NC:]
    stores = [pltpu.make_async_copy(err_v, err_ref, sems.at[4])]
    stores[0].start()
    for t in range(TB):
        for h in range(2):
            for a in range(h * HALF, (h + 1) * HALF):
                out = dot(factor_ref[t, h], chosen_ref[t, a], NN).astype(jnp.bfloat16)
                corr_v[t, 0, a] = out[:RHS]
                corr_v[t, 1, a] = out[RHS:]
            some = pl.ds(h * HALF, HALF)
            store = pltpu.make_async_copy(
                corr_v.at[t, :, some], corr_ref.at[t, :, some], sems.at[2 * t + h]
            )
            store.start()
            stores.append(store)
    for store in stores:
        store.wait()


def on_device(sizes, fine_residual, candidates, vector_pick, coarse_links):
    fine = fine_residual[0, 0, 0]
    pool = jnp.swapaxes(candidates[0, 0, 0], 2, 3)
    links = coarse_links[:, 0, 0]
    hbm = pl.BlockSpec(memory_space=pltpu.HBM)
    sides = len(SIDES)
    error, factor, chosen = pl.pallas_call(
        functools.partial(kernel, sizes),
        out_shape=(
            pltpu.VMEM((TB, RHS, LANES), jnp.float32),
            pltpu.VMEM((TB, 2, 2 * RHS, 2 * POOL), jnp.bfloat16),
            pltpu.VMEM((TB, DOF, 2 * POOL, SITES), jnp.bfloat16),
        ),
        in_specs=[hbm] * 4,
        out_specs=(pl.BlockSpec(memory_space=pltpu.VMEM),) * 3,
        scratch_shapes=[
            pltpu.VMEM((TB, 2, DOF, RHS, SITES), jnp.bfloat16),
            pltpu.VMEM((TB, POOL, DOF, 2, SITES), jnp.bfloat16),
            pltpu.VMEM((TB, 9, NC, LANES), jnp.float32),
            pltpu.VMEM((TB, 8 * LANES, LANES), jnp.bfloat16),
            pltpu.VMEM((TB, 8 * LANES, LANES), jnp.bfloat16),
            pltpu.VMEM((TB, RHS, LANES), jnp.float32),
            pltpu.VMEM((TB, RHS, LANES), jnp.float32),
            pltpu.VMEM((2, sides, TB, RHS, LANES), jnp.float32),
            pltpu.VMEM((1, NV), jnp.int32),
            pltpu.VMEM((2, 2, 2 * POOL, LANES), jnp.bfloat16),
            pltpu.VMEM((LANES, 4 * LANES), jnp.bfloat16),
            pltpu.SemaphoreType.DMA((6,)),
            pltpu.SemaphoreType.DMA((2, len(UNITS), sides)),
            pltpu.SemaphoreType.DMA((2, len(UNITS), sides)),
        ],
        compiler_params=pltpu.CompilerParams(
            collective_id=0, has_side_effects=True, vmem_limit_bytes=48 << 20
        ),
        name="coarse_correction",
    )(*[pltpu.with_memory_space_constraint(x, pltpu.HBM) for x in (vector_pick[None], fine, pool, links)])
    vmem = pl.BlockSpec(memory_space=pltpu.VMEM)
    correction, error = pl.pallas_call(
        prolong,
        out_shape=(
            pltpu.HBM((TB, 2, DOF, RHS, SITES), jnp.bfloat16),
            pltpu.HBM((TB, 2, RHS, NC), jnp.float32),
        ),
        in_specs=[vmem] * 3,
        out_specs=(hbm, hbm),
        scratch_shapes=[
            pltpu.VMEM((TB, 2, DOF, RHS, SITES), jnp.bfloat16),
            pltpu.VMEM((TB, 2, RHS, NC), jnp.float32),
            pltpu.SemaphoreType.DMA((5,)),
        ],
        compiler_params=pltpu.CompilerParams(vmem_limit_bytes=32 << 20),
        name="prolong",
    )(*[pltpu.with_memory_space_constraint(x, pltpu.VMEM) for x in (error, factor, chosen)])
    return (correction[None, None, None], jnp.swapaxes(error, 2, 3)[None, None, None])


def solution(mesh):
    placed = (
        P("gx", "gy", "gz", None, None, None, None, None),
        P("gx", "gy", "gz", None, None, None, None, None),
        P(),
        P(None, "gy", "gz", None, None, None, None),
    )
    return jax.shard_map(
        functools.partial(on_device, dict(mesh.shape)),
        mesh=mesh,
        in_specs=placed,
        out_specs=(
            P("gx", "gy", "gz", None, None, None, None, None),
            P("gx", "gy", "gz", None, None, None, None),
        ),
        check_vma=False,
    )
```
